32 devices in a mesh: depth: 8 (over z, x), col: 4 (over y, core).
Axes of the slice: x: 2, y: 2, z: 4, core: 2. Of those that a mesh axis runs over, the one named last changes fastest.
Arguments:
- voxel_bins: int32 [32, 128, 2048], P('depth', None, 'col'), may hold values from 0 to 4095
- color_table: bfloat16 [3, 256], replicated, may hold values from 0 to 2
- opacity_table: bfloat16 [256], replicated, may hold values from 0 to 0.125
- brick_order: int32 [8], replicated, may hold values from 0 to 7, as said below
Outputs:
- frame: float32 [4, 16, 8, 2048], P(None, None, 'depth', 'col')
The draws below stay inside these ranges and needn't reach their ends.
Inputs may be any that keep to these rules, and one draw needn't show every extreme that they name: brick_order is a monotone order of the bricks: either brick_order[b] = b for every b or brick_order[b] = 7 - b for every b.
All inputs are finite; a program needn't handle non-finite values.
Results may differ from the reference program's by a relative error of at most 0.0003.
Values sent between devices are 32-bit elements; how exact they have to be, the bound alone decides.
A program may use at most 192 MiB of HBM per device.

```python
import jax
import jax.numpy as jnp
from jax import lax

COLS = 2048
ROWS = 128
BINS = 256
QUANT_LEVELS = 4096
BRICKS = 8
SLICES = 32
STRIPE = 16


def draw_brick_order(key, part):
    flipped = jax.random.randint(jax.random.fold_in(key, 17), (), 0, 2)
    base = jnp.arange(BRICKS, dtype=jnp.int32)
    return jnp.where(flipped == 1, BRICKS - 1 - base, base).astype(jnp.int32)


def with_ends(array, stream_key, least, high):
    spot = [jax.random.randint(jax.random.fold_in(stream_key, axis), (), 0, length) for axis, length in enumerate(array.shape)]
    main_axis = array.shape.index(max(array.shape))
    next_to = spot[:main_axis] + [(spot[main_axis] + 1) % array.shape[main_axis]] + spot[main_axis + 1:]
    return array.at[tuple(spot)].set(least).at[tuple(next_to)].set(high)


def setup_inputs(seed: int = 0) -> dict:
    key_of = jax.random.split(jax.random.key(seed), 5)
    voxel_bins = with_ends(jax.random.randint(key_of[0], (SLICES, ROWS, COLS), 0, QUANT_LEVELS), jax.random.fold_in(key_of[0], 1), 0, QUANT_LEVELS - 1).astype(jnp.int32)
    color_table = jnp.clip(jax.random.uniform(key_of[1], (3, BINS), jnp.float32, 0.0, 2.0), 0.0, 2.0).astype(jnp.bfloat16)
    opacity_table = jnp.clip(jax.random.uniform(key_of[2], (BINS,), jnp.float32, 0.0, 0.125), 0.0, 0.125).astype(jnp.bfloat16)
    brick_order = draw_brick_order(jax.random.fold_in(key_of[4], 71), 0)
    return {"voxel_bins": voxel_bins, "color_table": color_table, "opacity_table": opacity_table, "brick_order": brick_order}


light_depth = 0.48
light_rows = 0.6
light_cols = 0.64

def part_of(field, start, stop, dimension):
    return lax.slice_in_dim(field, start, stop, axis=dimension)

def smooth_valid(field, dimension):
    length = field.shape[dimension]
    return part_of(field, 0, length - 2, dimension) + 2.0 * part_of(field, 1, length - 1, dimension) + part_of(field, 2, length, dimension)

def differ_valid(field, dimension):
    length = field.shape[dimension]
    return part_of(field, 2, length, dimension) - part_of(field, 0, length - 2, dimension)

def shifted(field, dimension, offset):
    length = field.shape[dimension]
    zero_shape = list(field.shape)
    zero_shape[dimension] = 1
    zero_rows = jnp.zeros(zero_shape, field.dtype)
    if offset > 0:
        return jnp.concatenate([zero_rows, part_of(field, 0, length - 1, dimension)], axis=dimension)
    return jnp.concatenate([part_of(field, 1, length, dimension), zero_rows], axis=dimension)

def smooth_same(field, dimension):
    return shifted(field, dimension, 1) + 2.0 * field + shifted(field, dimension, -1)

def differ_same(field, dimension):
    return shifted(field, dimension, -1) - shifted(field, dimension, 1)

def gradient(padded):
    grad_depth = smooth_valid(smooth_same(differ_valid(padded, 0), 1), 2)
    grad_rows = smooth_valid(smooth_valid(differ_same(padded, 1), 0), 2)
    grad_cols = smooth_same(smooth_valid(differ_valid(padded, 2), 0), 1)
    return (grad_depth, grad_rows, grad_cols)

def build_table(color_table, opacity_table):
    lower_table = jnp.concatenate([color_table, opacity_table[None, :]], axis=0)
    upper_table = jnp.concatenate([lower_table[:, 1:], lower_table[:, -1:]], axis=1)
    return jnp.concatenate([lower_table, upper_table], axis=0)

def samples_of(bins_block, grad_depth, grad_rows, grad_cols, table_pairs):
    levels = QUANT_LEVELS - 1
    scaled = bins_block * (BINS - 1)
    lower_bin = (scaled // levels).astype(jnp.int32)
    fraction = (scaled - lower_bin * levels).astype(jnp.float32) / float(levels)
    values = jnp.take(table_pairs, lower_bin, axis=1).astype(jnp.float32)
    interpolated = values[:4] * (1.0 - fraction) + values[4:] * fraction
    facing = light_depth * grad_depth + light_rows * grad_rows + light_cols * grad_cols
    magnitude = grad_depth * grad_depth + grad_rows * grad_rows + grad_cols * grad_cols
    shading = 0.2 + 0.8 * jnp.abs(facing) / jnp.sqrt(magnitude + 1.0)
    opacity = interpolated[3]
    colour = interpolated[:3] * (shading * opacity)[None]
    return jnp.concatenate([colour, opacity[None]], axis=0)

def reference(voxel_bins, color_table, opacity_table, brick_order):
    table_pairs = build_table(color_table, opacity_table)
    ascending = brick_order[0] < brick_order[BRICKS - 1]

    def advance(accumulated, position):
        slab_index = jnp.where(ascending, position, SLICES - 1 - position).astype(jnp.int32)
        layers = []
        for offset in (-1, 0, 1):
            target = slab_index + offset
            inside = jnp.logical_and(target >= 0, target < SLICES)
            clamped = jnp.clip(target, 0, SLICES - 1).astype(jnp.int32)
            layer = lax.dynamic_slice_in_dim(voxel_bins, clamped, 1, 0)
            layers.append(layer.astype(jnp.float32) / float(QUANT_LEVELS - 1) * inside.astype(jnp.float32))
        stacked = jnp.concatenate(layers, axis=0)
        padded = jnp.pad(stacked, ((0, 0), (0, 0), (1, 1)))
        grad_depth, grad_rows, grad_cols = gradient(padded)
        centre = lax.dynamic_slice_in_dim(voxel_bins, slab_index, 1, 0)
        sample = samples_of(centre, grad_depth, grad_rows, grad_cols, table_pairs)[:, 0]
        return (accumulated + (1.0 - accumulated[3:4]) * sample, None)
    start = jnp.zeros((4, ROWS, COLS), jnp.float32)
    accumulated, unused = lax.scan(advance, start, jnp.arange(SLICES, dtype=jnp.int32))
    return accumulated.reshape(4, STRIPE, BRICKS, COLS)
```

```python
import functools

import jax
import jax.numpy as jnp
from jax import lax
from jax.experimental import pallas as pl
from jax.experimental.pallas import tpu as pltpu
from jax.sharding import PartitionSpec as P

BINS = 256
LEVELS = 4095.0
LIGHT = (0.48, 0.6, 0.64)
GROUP = 8


def planes(v_ref, k, c):
    lo, mid, hi = v_ref[k, c], v_ref[k, c + 1], v_ref[k, c + 2]
    width = lo.shape[-1]
    cols = width - 128
    smooth = lo + 2.0 * mid + hi
    differ = hi - lo
    s_left, s_right = pltpu.roll(smooth, 1, 1)[:, :cols], pltpu.roll(smooth, width - 1, 1)[:, :cols]
    d_left, d_right = pltpu.roll(differ, 1, 1)[:, :cols], pltpu.roll(differ, width - 1, 1)[:, :cols]
    a = s_left + 2.0 * smooth[:, :cols] + s_right
    b = d_left + 2.0 * differ[:, :cols] + d_right
    g = s_right - s_left
    return a, b, g


def lookup(tables, voxels):
    outs = [[] for _ in range(4)]
    for j in range(voxels.shape[1] // 128):
        v = voxels[:, j * 128 : (j + 1) * 128]
        scaled = v * 17.0
        lower = jnp.floor((scaled + 0.5) * (1.0 / 273.0))
        fraction = (scaled - lower * 273.0) * (1.0 / 273.0)
        index = lower.astype(jnp.int32)
        high = index >= 128
        lane = jnp.bitwise_and(index, 127)
        for q in range(4):
            base = jnp.where(
                high,
                jnp.take_along_axis(tables[q][1], lane, axis=1),
                jnp.take_along_axis(tables[q][0], lane, axis=1),
            )
            step = jnp.where(
                high,
                jnp.take_along_axis(tables[q + 4][1], lane, axis=1),
                jnp.take_along_axis(tables[q + 4][0], lane, axis=1),
            )
            outs[q].append(base + fraction * step)
    return [jnp.concatenate(o, axis=1) for o in outs]


def load_tables(tab_ref):
    return [
        [jnp.broadcast_to(tab_ref[q : q + 1, h * 128 : (h + 1) * 128], (8, 128)) for h in range(2)]
        for q in range(8)
    ]


def composite_tile(v_ref, tab_ref, c, slices):
    tables = load_tables(tab_ref)
    cols = v_ref.shape[-1] - 128
    ascending = jnp.broadcast_to(tab_ref[8:9, 0:1], (8, cols)) > 0.5
    before = planes(v_ref, 0, c)
    here = planes(v_ref, 1, c)
    acc = [jnp.zeros((8, cols), jnp.float32)] * 4
    for k in range(1, slices + 1):
        after = planes(v_ref, k + 1, c)
        gd = after[0] - before[0]
        gr = before[1] + 2.0 * here[1] + after[1]
        gc = before[2] + 2.0 * here[2] + after[2]
        facing = LIGHT[0] * gd + LIGHT[1] * gr + LIGHT[2] * gc
        magnitude = gd * gd + gr * gr + gc * gc
        shading = 0.2 + 0.8 * jnp.abs(facing) * lax.rsqrt(magnitude + LEVELS * LEVELS)
        red, green, blue, opacity = lookup(tables, v_ref[k, c + 1][:, :cols])
        weight = shading * opacity
        new = [red * weight, green * weight, blue * weight, opacity]
        trans = 1.0 - jnp.where(ascending, acc[3], opacity)
        acc = [
            jnp.where(ascending, a, n) + trans * jnp.where(ascending, n, a)
            for a, n in zip(acc, new)
        ]
        before, here = here, after
    return acc


def local_kernel(slices, v_ref, tab_ref, out_ref):
    def step(c, carry):
        acc = composite_tile(v_ref, tab_ref, c, slices)
        for q in range(4):
            out_ref[c, q] = acc[q]
        return carry

    lax.fori_loop(0, GROUP, step, 0)


def build_tables(color_table, opacity_table, brick_order):
    lower = jnp.concatenate([color_table, opacity_table[None]], axis=0).astype(jnp.float32)
    upper = jnp.concatenate([lower[:, 1:], lower[:, -1:]], axis=1)
    asc = (brick_order[0] < brick_order[-1]).astype(jnp.float32)
    return jnp.concatenate(
        [lower, upper - lower, jnp.full((8, BINS), asc, jnp.float32)], axis=0
    )


def shift_perm(axis, distance):
    n = lax.axis_size(axis)
    return [(i, i + distance) for i in range(n) if 0 <= i + distance < n]


def swap(x, bit):
    return lax.ppermute(x, "depth", [(i, i ^ bit) for i in range(lax.axis_size("depth"))])


def over(front, back, axis):
    alpha = lax.slice_in_dim(front, 3, 4, axis=axis)
    return front + (1.0 - alpha) * back


def body(voxel_bins, color_table, opacity_table, brick_order):
    me = lax.axis_index("depth")
    n = lax.axis_size("depth")
    odd = me % 2 == 1
    slices, rows, cols = voxel_bins.shape
    half = rows // 2
    tiles = half // GROUP
    v = voxel_bins.astype(jnp.float32)
    zero = jnp.zeros((slices, 1, cols), jnp.float32)
    top = jnp.concatenate([zero, v[:, : half + 1]], axis=1)
    bottom = jnp.concatenate([v[:, half - 1 :], zero], axis=1)
    mine = jnp.where(odd, bottom, top)
    theirs = swap(jnp.where(odd, top, bottom), 1)
    pair = jnp.concatenate([jnp.where(odd, theirs, mine), jnp.where(odd, mine, theirs)], axis=0)
    from_before = lax.ppermute(pair[-1:], "depth", shift_perm("depth", 2))
    from_after = lax.ppermute(pair[:1], "depth", shift_perm("depth", -2))
    pair = jnp.concatenate([from_before, pair, from_after], axis=0)
    from_left = lax.ppermute(pair[:, :, -128:], "col", shift_perm("col", 1))
    from_right = lax.ppermute(pair[:, :, :128], "col", shift_perm("col", -1))
    edge = jnp.where(jnp.arange(128) < 64, from_right, from_left)
    pair = jnp.concatenate([pair, edge], axis=2)
    ext = jnp.stack(
        [pair[:, c : c + 8 * (tiles - 1) + 1 : 8] for c in range(GROUP + 2)], axis=1
    )
    tab = build_tables(color_table, opacity_table, brick_order)
    part = pl.pallas_call(
        functools.partial(local_kernel, 2 * slices),
        out_shape=jax.ShapeDtypeStruct((GROUP, 4, tiles, cols), jnp.float32),
        in_specs=[pl.BlockSpec(memory_space=pltpu.VMEM)] * 2,
        out_specs=pl.BlockSpec(memory_space=pltpu.VMEM),
        compiler_params=pltpu.CompilerParams(vmem_limit_bytes=40 * 2**20),
    )(ext, tab)
    ascending = brick_order[0] < brick_order[-1]
    part = part.reshape(2, 2, 2, 4, tiles, cols)
    for axis, bit in ((1, 2), (0, 4)):
        set_bit = me // bit % 2 == 1
        first, second = jnp.take(part, 0, axis=axis), jnp.take(part, 1, axis=axis)
        part = jnp.expand_dims(jnp.where(set_bit, second, first), axis)
        got = jnp.expand_dims(swap(jnp.where(set_bit, first, second), bit), axis)
        front = set_bit != ascending
        part = jnp.where(front, over(part, got, 3), over(got, part, 3))
    part = part.reshape(2, 4, tiles, cols)
    keep = jnp.where(odd, part[1], part[0])
    got = swap(jnp.where(odd, part[0], part[1]), 1)
    picture = jnp.where(
        odd, jnp.concatenate([got, keep], axis=1), jnp.concatenate([keep, got], axis=1)
    )
    return finish(picture, ascending, me, n)


def finish(picture, ascending, me, n):
    bit = GROUP
    while bit < n:
        count = picture.shape[1]
        halves = picture.reshape(4, count // 2, 2, picture.shape[2])
        set_bit = me // bit % 2 == 1
        keep = jnp.where(set_bit, halves[:, :, 1], halves[:, :, 0])
        got = swap(jnp.where(set_bit, halves[:, :, 0], halves[:, :, 1]), bit)
        picture = jnp.where(set_bit != ascending, over(keep, got, 0), over(got, keep, 0))
        bit *= 2
    return picture[:, :, None, :]


def solution(mesh):
    in_specs = (P("depth", None, "col"), P(), P(), P())
    out_specs = P(None, None, "depth", "col")
    return jax.shard_map(body, mesh=mesh, in_specs=in_specs, out_specs=out_specs, check_vma=False)
```

```python
import functools

import jax
import jax.numpy as jnp
from jax import lax
from jax.experimental import pallas as pl
from jax.experimental.pallas import tpu as pltpu
from jax.sharding import PartitionSpec as P

BINS = 256
LEVELS = 4095.0
LIGHT = (0.48, 0.6, 0.64)
GROUP = 8
CHUNKS = ((0, 4), (4, 6), (6, 9), (9, 10))
READY = ((0, 0), (0, 2), (2, 5), (5, 8))
EXT = GROUP + 2
MESH = pl.DeviceIdType.MESH


def planes(ext, right, left, k, c):
    def tile(step):
        at = lax.rem(c + 2 + step, EXT)
        lane = lax.broadcasted_iota(jnp.int32, (8, 128), 1)
        edge = jnp.where(lane < 64, right[k, at], left[k, at])
        return jnp.concatenate([ext[k, at], edge], axis=1)

    lo, mid, hi = tile(0), tile(1), tile(2)
    width = lo.shape[-1]
    cols = width - 128
    smooth = lo + 2.0 * mid + hi
    differ = hi - lo
    s_left, s_right = pltpu.roll(smooth, 1, 1)[:, :cols], pltpu.roll(smooth, width - 1, 1)[:, :cols]
    d_left, d_right = pltpu.roll(differ, 1, 1)[:, :cols], pltpu.roll(differ, width - 1, 1)[:, :cols]
    a = s_left + 2.0 * smooth[:, :cols] + s_right
    b = d_left + 2.0 * differ[:, :cols] + d_right
    g = s_right - s_left
    return a, b, g


def lookup(tables, voxels):
    outs = [[] for _ in range(4)]
    for j in range(voxels.shape[1] // 128):
        v = voxels[:, j * 128 : (j + 1) * 128]
        scaled = v * 17.0
        lower = jnp.floor((scaled + 0.5) * (1.0 / 273.0))
        fraction = (scaled - lower * 273.0) * (1.0 / 273.0)
        index = lower.astype(jnp.int32)
        high = index >= 128
        lane = jnp.bitwise_and(index, 127)
        for q in range(4):
            base = jnp.where(
                high,
                jnp.take_along_axis(tables[q][1], lane, axis=1),
                jnp.take_along_axis(tables[q][0], lane, axis=1),
            )
            step = jnp.where(
                high,
                jnp.take_along_axis(tables[q + 4][1], lane, axis=1),
                jnp.take_along_axis(tables[q + 4][0], lane, axis=1),
            )
            outs[q].append(base + fraction * step)
    return [jnp.concatenate(o, axis=1) for o in outs]


def load_tables(tab_ref):
    return [
        [jnp.broadcast_to(tab_ref[q : q + 1, h * 128 : (h + 1) * 128], (8, 128)) for h in range(2)]
        for q in range(8)
    ]


def blend(ascending, acc, new):
    trans = 1.0 - jnp.where(ascending, acc[3], new[3])
    return [
        jnp.where(ascending, a, n) + trans * jnp.where(ascending, n, a) for a, n in zip(acc, new)
    ]


def composite_tile(ext, right, left, tab_ref, ascending, c, slices):
    tables = load_tables(tab_ref)
    before = planes(ext, right, left, 0, c)
    here = planes(ext, right, left, 1, c)
    acc = None
    for k in range(1, slices + 1):
        after = planes(ext, right, left, k + 1, c)
        gd = after[0] - before[0]
        gr = before[1] + 2.0 * here[1] + after[1]
        gc = before[2] + 2.0 * here[2] + after[2]
        facing = LIGHT[0] * gd + LIGHT[1] * gr + LIGHT[2] * gc
        magnitude = gd * gd + gr * gr + gc * gc
        shading = 0.2 + 0.8 * jnp.abs(facing) * lax.rsqrt(magnitude + LEVELS * LEVELS)
        red, green, blue, opacity = lookup(tables, ext[k, lax.rem(c + 3, EXT)])
        weight = shading * opacity
        new = [red * weight, green * weight, blue * weight, opacity]
        acc = new if acc is None else blend(ascending, acc, new)
        before, here = here, after
    return acc


def render_kernel(
    nd, nc, vox, tab_ref, out_ref, rows_pad, ext, right, left, sent, sent_rows, got_rows,
    part, inbox, last_out, last_in, x_send, x_recv, h_send, h_recv,
    p_send, p_recv, f_send, f_recv,
):
    slices, rows, cols = vox.shape
    half = rows // 2
    d, col = lax.axis_index("depth"), lax.axis_index("col")
    x = lax.rem(d, 2)
    z = lax.rem(d, GROUP) // 2
    base = d - lax.rem(d, GROUP)
    odd = x == 1
    partner = d + 1 - 2 * x
    own = 1 + slices * x
    other = 1 + slices * (1 - x)
    first_k, last_k, end_k = 1, 2 * slices, 2 * slices + 1
    near_k = first_k + (last_k - first_k) * x
    far_k = last_k + (first_k - last_k) * x
    near_d = d - 2 + 4 * x
    far_d = d + 2 - 4 * x
    near_dst = end_k - end_k * x
    far_dst = end_k * x
    near_ok = jnp.logical_and(near_d >= 0, near_d < nd)
    far_ok = jnp.logical_and(far_d >= 0, far_d < nd)
    left_ok, right_ok = col > 0, col < nc - 1
    both = jnp.logical_and

    barrier = pltpu.get_barrier_semaphore()

    def greet(device, column, ok):
        @pl.when(ok)
        def _():
            pl.semaphore_signal(barrier, inc=1, device_id=(device, column), device_id_type=MESH)

        return jnp.where(ok, 1, 0)

    count = greet(partner, col, d >= 0)
    for step, ok in ((-1, left_ok), (1, right_ok)):
        count += greet(d, col + step, ok)
    for device, ok in ((near_d, near_ok), (far_d, far_ok)):
        count += greet(device, col, ok)
        for step, side in ((-1, left_ok), (1, right_ok)):
            count += greet(device, col + step, both(ok, side))
    for j in range(GROUP // 2):
        count += greet(base + 2 * j + x, col, z != j)

    pad = jnp.zeros((8, 128), jnp.float32)
    blocks = cols // 128

    def convert(k, carry):
        for j in range(blocks):
            lanes = slice(j * 128, j * 128 + 128)
            rows_pad[k, j, 0:8] = pad
            rows_pad[k, j, rows + 8 : rows + 16] = pad
            rows_pad[k, j, 8 : rows + 8] = vox[k, :, lanes].astype(jnp.float32)
            for c in range(EXT):
                at = (c + 2) % EXT
                upper = rows_pad[k, j, pl.ds(7 + c, 8, stride=8), :]
                lower = rows_pad[k, j, pl.ds(7 + c + half, 8, stride=8), :]
                ext[own + k, at, :, lanes] = jnp.where(odd, lower, upper)
                if 0 < c < EXT - 1:
                    sent[k, at, :, lanes] = jnp.where(odd, upper, lower)
        return carry

    lax.fori_loop(0, slices, convert, 0)
    for k in range(slices):
        for spot, up, low in ((k, 7, 7 + half), (slices + k, 8 + half, 8 + rows)):
            for j in range(blocks):
                sent_rows[spot : spot + 1, j * 128 : j * 128 + 128] = jnp.where(
                    odd, rows_pad[k, j, up : up + 1, :], rows_pad[k, j, low : low + 1, :]
                )

    def clear(ref, k):
        def one(i, carry):
            ref[k, i] = jnp.zeros(ref.shape[2:], jnp.float32)
            return carry

        lax.fori_loop(0, EXT, one, 0)

    for ok, k in ((far_ok, near_dst), (near_ok, far_dst)):
        @pl.when(jnp.logical_not(ok))
        def _(k=k):
            for ref in (ext, right, left):
                clear(ref, k)
    for ref, ok in ((right, right_ok), (left, left_ok)):
        @pl.when(jnp.logical_not(ok))
        def _(ref=ref):
            def every(k, carry):
                clear(ref, k)
                return carry

            lax.fori_loop(0, end_k + 1, every, 0)

    def remote(src, dst, ssem, rsem, device, column):
        return pltpu.make_async_remote_copy(
            src_ref=src, dst_ref=dst, send_sem=ssem, recv_sem=rsem,
            device_id=(device, column), device_id_type=MESH,
        )

    def halo_copies(h, start, k, dst, device, to_ok, from_ok, a, b):
        span = pl.ds(a, b - a)
        four = pl.ds(start, slices)
        first, last = pl.ds(0, 128), pl.ds(cols - 128, 128)
        entries = [
            (ext.at[k, span], ext.at[dst, span], device, col, to_ok, from_ok),
            (ext.at[four, span, :, first], right.at[four, span], d, col - 1, left_ok, right_ok),
            (ext.at[four, span, :, last], left.at[four, span], d, col + 1, right_ok, left_ok),
            (ext.at[k, span, :, first], right.at[dst, span], device, col - 1,
             both(to_ok, left_ok), both(from_ok, right_ok)),
            (ext.at[k, span, :, last], left.at[dst, span], device, col + 1,
             both(to_ok, right_ok), both(from_ok, left_ok)),
        ]
        return [
            (remote(s, t, h_send.at[h, i], h_recv.at[h, i], device, column), to, fr)
            for i, (s, t, device, column, to, fr) in enumerate(entries)
        ]

    def start_all(entries):
        for copy, to, _ in entries:
            pl.when(to)(copy.start)

    def receive_all(entries):
        for copy, _, fr in entries:
            pl.when(fr)(copy.wait_recv)

    pl.semaphore_wait(barrier, count)

    x_groups, number = [], 0
    for q, (lo, hi) in enumerate(CHUNKS):
        group = []
        for a, b in ((0, 1), (3, 4)) if q == 0 else ((lo, hi),):
            span = pl.ds(a, b - a)
            group.append(remote(
                sent.at[:, span], ext.at[pl.ds(own, slices), span],
                x_send.at[number], x_recv.at[number], partner, col,
            ))
            number += 1
        x_groups.append(group)
    x_groups[0].append(
        remote(sent_rows, got_rows, x_send.at[number], x_recv.at[number], partner, col)
    )
    whole = halo_copies(0, own, near_k, near_dst, near_d, near_ok, far_ok, 0, EXT)
    for copy in x_groups[0]:
        copy.start()
    start_all(whole)
    for group in x_groups[1:]:
        for copy in group:
            copy.start()

    ascending = jnp.broadcast_to(tab_ref[8:9, 0:1], (8, cols)) > 0.5
    row = lax.broadcasted_iota(jnp.int32, (8, cols), 0)

    def to_device(c):
        j, parity = c // 2, lax.rem(c, 2)
        return remote(
            part.at[c], inbox.at[parity, z], p_send.at[c], p_recv.at[parity, z],
            base + 2 * j + x, col,
        )

    def render(c, carry):
        acc = composite_tile(ext, right, left, tab_ref, ascending, c, 2 * slices)
        mine = c // 2 == z

        @pl.when(mine)
        def _():
            for i in range(4):
                inbox[lax.rem(c, 2), z, i] = acc[i]

        @pl.when(jnp.logical_not(mine))
        def _():
            for i in range(4):
                part[c, i] = acc[i]
            to_device(c).start()

        return carry

    forwards = []
    for q, (lo, hi) in enumerate(CHUNKS):
        for copy in x_groups[q]:
            copy.wait_recv()
        if q == 0:
            for k in range(slices):
                above = pltpu.roll(ext[other + k, 0], 1, 0)
                below = pltpu.roll(ext[other + k, 3], 7, 0)
                ext[other + k, 2] = jnp.where(row == 0, got_rows[k : k + 1, :], above)
                ext[other + k, 1] = jnp.where(
                    row == 7, got_rows[slices + k : slices + k + 1, :], below
                )
        ahead = halo_copies(1 + q, other, far_k, far_dst, far_d, far_ok, near_ok, lo, hi)
        start_all(ahead)
        forwards.append(ahead)
        if q == 0:
            receive_all(whole)
        else:
            receive_all(forwards[q - 1])
            lax.fori_loop(*READY[q - 1], render, 0)
    receive_all(forwards[-1])
    lax.fori_loop(*READY[-1], render, 0)

    def gathered(parity):
        for j in range(GROUP // 2):
            @pl.when(z != j)
            def _(j=j):
                remote(
                    part.at[0], inbox.at[parity, j], p_send.at[0], p_recv.at[parity, j],
                    partner, col,
                ).wait_recv()
        acc = None
        for j in range(GROUP // 2):
            new = [inbox[parity, j, i] for i in range(4)]
            acc = new if acc is None else blend(ascending, acc, new)
        return acc

    for i, value in enumerate(gathered(1 - x)):
        last_out[i] = value
    last = remote(last_out, last_in, f_send, f_recv, partner, col)
    last.start()
    for i, value in enumerate(gathered(x)):
        out_ref[i, pl.ds(pl.multiple_of(8 * x, 8), 8), :] = value
    last.wait_recv()
    for i in range(4):
        out_ref[i, pl.ds(pl.multiple_of(8 - 8 * x, 8), 8), :] = last_in[i]

    last.wait_send()
    for group in x_groups:
        for copy in group:
            copy.wait_send()
    for entries in [whole] + forwards:
        for copy, to, _ in entries:
            pl.when(to)(copy.wait_send)

    def drain(c, carry):
        @pl.when(c // 2 != z)
        def _():
            to_device(c).wait_send()

        return carry

    lax.fori_loop(0, GROUP, drain, 0)


def build_tables(color_table, opacity_table, brick_order):
    lower = jnp.concatenate([color_table, opacity_table[None]], axis=0).astype(jnp.float32)
    upper = jnp.concatenate([lower[:, 1:], lower[:, -1:]], axis=1)
    asc = (brick_order[0] < brick_order[-1]).astype(jnp.float32)
    return jnp.concatenate(
        [lower, upper - lower, jnp.full((8, BINS), asc, jnp.float32)], axis=0
    )


def swap(x, bit):
    return lax.ppermute(x, "depth", [(i, i ^ bit) for i in range(lax.axis_size("depth"))])


def over(front, back, axis):
    alpha = lax.slice_in_dim(front, 3, 4, axis=axis)
    return front + (1.0 - alpha) * back


def body(voxel_bins, color_table, opacity_table, brick_order):
    me = lax.axis_index("depth")
    n = lax.axis_size("depth")
    slices, rows, cols = voxel_bins.shape
    tiles = rows // GROUP
    tab = build_tables(color_table, opacity_table, brick_order)
    depth = 2 * slices + 2
    vmem = lambda *shape: pltpu.VMEM(shape, jnp.float32)
    dma = lambda *shape: pltpu.SemaphoreType.DMA(shape)
    chunks = len(CHUNKS)
    picture = pl.pallas_call(
        functools.partial(render_kernel, n, lax.axis_size("col")),
        out_shape=jax.ShapeDtypeStruct((4, tiles, cols), jnp.float32),
        in_specs=[pl.BlockSpec(memory_space=pltpu.VMEM)] * 2,
        out_specs=pl.BlockSpec(memory_space=pltpu.VMEM),
        scratch_shapes=[
            vmem(slices, cols // 128, rows + 16, 128),
            vmem(depth, EXT, 8, cols),
            vmem(depth, EXT, 8, 128),
            vmem(depth, EXT, 8, 128),
            vmem(slices, EXT, 8, cols),
            vmem(2 * slices, cols),
            vmem(2 * slices, cols),
            vmem(GROUP, 4, 8, cols),
            vmem(2, GROUP // 2, 4, 8, cols),
            vmem(4, 8, cols),
            vmem(4, 8, cols),
            dma(chunks + 2),
            dma(chunks + 2),
            dma(chunks + 1, 5),
            dma(chunks + 1, 5),
            dma(GROUP),
            dma(2, GROUP // 2),
            pltpu.SemaphoreType.DMA,
            pltpu.SemaphoreType.DMA,
        ],
        compiler_params=pltpu.CompilerParams(
            collective_id=0, has_side_effects=True, vmem_limit_bytes=40 * 2**20
        ),
    )(voxel_bins, tab)
    ascending = brick_order[0] < brick_order[-1]
    return finish(picture, ascending, me, n)


def finish(picture, ascending, me, n):
    bit = GROUP
    while bit < n:
        count = picture.shape[1]
        halves = picture.reshape(4, count // 2, 2, picture.shape[2])
        set_bit = me // bit % 2 == 1
        keep = jnp.where(set_bit, halves[:, :, 1], halves[:, :, 0])
        got = swap(jnp.where(set_bit, halves[:, :, 0], halves[:, :, 1]), bit)
        picture = jnp.where(set_bit != ascending, over(keep, got, 0), over(got, keep, 0))
        bit *= 2
    return picture[:, :, None, :]


def solution(mesh):
    in_specs = (P("depth", None, "col"), P(), P(), P())
    out_specs = P(None, None, "depth", "col")
    return jax.shard_map(body, mesh=mesh, in_specs=in_specs, out_specs=out_specs, check_vma=False)
```

```python
import functools

import jax
import jax.numpy as jnp
from jax import lax
from jax.experimental import pallas as pl
from jax.experimental.pallas import tpu as pltpu
from jax.sharding import PartitionSpec as P

BINS = 256
LEVELS = 4095.0
LIGHT = (0.48, 0.6, 0.64)
GROUP = 8
CHUNKS = GROUP - 1
EXT = GROUP + 2
MESH = pl.DeviceIdType.MESH


def planes(ext, edges, k, c):
    def tile(step):
        at = lax.rem(c + 2 + step, EXT)
        return jnp.concatenate([ext[k, at], edges[k, at]], axis=1)

    lo, mid, hi = tile(0), tile(1), tile(2)
    width = lo.shape[-1]
    cols = width - 128
    smooth = lo + 2.0 * mid + hi
    differ = hi - lo
    s_left, s_right = pltpu.roll(smooth, 1, 1)[:, :cols], pltpu.roll(smooth, width - 1, 1)[:, :cols]
    d_left, d_right = pltpu.roll(differ, 1, 1)[:, :cols], pltpu.roll(differ, width - 1, 1)[:, :cols]
    a = s_left + 2.0 * smooth[:, :cols] + s_right
    b = d_left + 2.0 * differ[:, :cols] + d_right
    g = s_right - s_left
    return a, b, g


def lookup(tables, voxels):
    outs = [[] for _ in range(4)]
    for j in range(voxels.shape[1] // 128):
        v = voxels[:, j * 128 : (j + 1) * 128]
        scaled = v * 17.0
        lower = jnp.floor((scaled + 0.5) * (1.0 / 273.0))
        fraction = (scaled - lower * 273.0) * (1.0 / 273.0)
        index = lower.astype(jnp.int32)
        high = index >= 128
        lane = jnp.bitwise_and(index, 127)
        for q in range(4):
            base = jnp.where(
                high,
                jnp.take_along_axis(tables[q][1], lane, axis=1),
                jnp.take_along_axis(tables[q][0], lane, axis=1),
            )
            step = jnp.where(
                high,
                jnp.take_along_axis(tables[q + 4][1], lane, axis=1),
                jnp.take_along_axis(tables[q + 4][0], lane, axis=1),
            )
            outs[q].append(base + fraction * step)
    return [jnp.concatenate(o, axis=1) for o in outs]


def load_tables(tab_ref):
    return [
        [jnp.broadcast_to(tab_ref[q : q + 1, h * 128 : (h + 1) * 128], (8, 128)) for h in range(2)]
        for q in range(8)
    ]


def blend(ascending, acc, new):
    trans = 1.0 - jnp.where(ascending, acc[3], new[3])
    return [
        jnp.where(ascending, a, n) + trans * jnp.where(ascending, n, a) for a, n in zip(acc, new)
    ]


def composite_tile(ext, edges, tab_ref, ascending, c, slices):
    tables = load_tables(tab_ref)
    before = planes(ext, edges, 0, c)
    here = planes(ext, edges, 1, c)
    acc = None
    for k in range(1, slices + 1):
        after = planes(ext, edges, k + 1, c)
        gd = after[0] - before[0]
        gr = before[1] + 2.0 * here[1] + after[1]
        gc = before[2] + 2.0 * here[2] + after[2]
        facing = LIGHT[0] * gd + LIGHT[1] * gr + LIGHT[2] * gc
        magnitude = gd * gd + gr * gr + gc * gc
        shading = 0.2 + 0.8 * jnp.abs(facing) * lax.rsqrt(magnitude + LEVELS * LEVELS)
        red, green, blue, opacity = lookup(tables, ext[k, lax.rem(c + 3, EXT)])
        weight = shading * opacity
        new = [red * weight, green * weight, blue * weight, opacity]
        acc = new if acc is None else blend(ascending, acc, new)
        before, here = here, after
    return acc


def render_kernel(
    nd, nc, vox_hbm, color, opacity, order, out_ref, vox, tab_ref, rows_pad, ext, halos, edges,
    own_edges, from_right, from_left, sent_edges, sent, sent_rows, got_rows,
    part, inbox, last_out, last_in, v_sem, x_send, x_recv, h_send, h_recv, c_send, c_recv,
    p_send, p_recv, f_send, f_recv,
):
    slices, rows, cols = vox.shape
    half = rows // 2
    d, col = lax.axis_index("depth"), lax.axis_index("col")
    x = lax.rem(d, 2)
    z = lax.rem(d, GROUP) // 2
    base = d - lax.rem(d, GROUP)
    odd = x == 1
    partner = d + 1 - 2 * x
    own = 1 + slices * x
    other = 1 + slices * (1 - x)
    first_k, last_k, end_k = 1, 2 * slices, 2 * slices + 1
    near_k = first_k + (last_k - first_k) * x
    far_k = last_k + (first_k - last_k) * x
    near_d = d - 2 + 4 * x
    far_d = d + 2 - 4 * x
    near_dst = end_k - end_k * x
    far_dst = end_k * x
    near_ok = jnp.logical_and(near_d >= 0, near_d < nd)
    far_ok = jnp.logical_and(far_d >= 0, far_d < nd)
    left_ok, right_ok = col > 0, col < nc - 1

    loads = [
        pltpu.make_async_copy(vox_hbm.at[k], vox.at[k], v_sem.at[k]) for k in range(slices)
    ]
    for load in loads:
        load.start()
    barrier = pltpu.get_barrier_semaphore()

    def greet(device, column, ok):
        @pl.when(ok)
        def _():
            pl.semaphore_signal(barrier, inc=1, device_id=(device, column), device_id_type=MESH)

        return jnp.where(ok, 1, 0)

    count = greet(partner, col, d >= 0)
    for step, ok in ((-1, left_ok), (1, right_ok)):
        count += greet(d, col + step, ok)
    for device, ok in ((near_d, near_ok), (far_d, far_ok)):
        count += greet(device, col, ok)
    for j in range(GROUP // 2):
        count += greet(base + 2 * j + x, col, z != j)

    pad = jnp.zeros((8, 128), jnp.float32)
    blocks = cols // 128

    lower_table = jnp.concatenate(
        [color[...].astype(jnp.float32), opacity[...].astype(jnp.float32)], axis=0
    )
    bins = lower_table.shape[1]
    entry = lax.broadcasted_iota(jnp.int32, (4, bins), 1)
    upper_table = jnp.where(
        entry == bins - 1, lower_table, jnp.concatenate([lower_table[:, 1:], lower_table[:, :1]], 1)
    )
    tab_ref[0:4] = lower_table
    tab_ref[4:8] = upper_table - lower_table
    lane = lax.broadcasted_iota(jnp.int32, (8, 128), 1)

    def convert(k):
        pack, pack_sent = pad, pad
        for j in range(blocks):
            lanes = slice(j * 128, j * 128 + 128)
            rows_pad[k, j, 0:8] = pad
            rows_pad[k, j, rows + 8 : rows + 16] = pad
            rows_pad[k, j, 8 : rows + 8] = vox[k, :, lanes].astype(jnp.float32)
            for c in range(EXT):
                at = (c + 2) % EXT
                upper = rows_pad[k, j, pl.ds(7 + c, 8, stride=8), :]
                lower = rows_pad[k, j, pl.ds(7 + c + half, 8, stride=8), :]
                ext[own + k, at, :, lanes] = jnp.where(odd, lower, upper)
                here = jnp.where(odd, lower, upper)
                there = jnp.where(odd, upper, lower)
                for spot, block in ((2 * at, 0), ((2 * at + 127) % 128, blocks - 1)):
                    if j == block:
                        pack = jnp.where(lane == spot, pltpu.roll(here, 2 * at, 1), pack)
                        pack_sent = jnp.where(lane == spot, pltpu.roll(there, 2 * at, 1), pack_sent)
                if 0 < c < EXT - 1:
                    sent[k, at, :, lanes] = jnp.where(odd, upper, lower)
        own_edges[k] = pack
        own_edges[slices + k] = pack_sent

    for k in range(slices):
        loads[k].wait()
        convert(k)
    for k in range(slices):
        for spot, up, low in ((k, 7, 7 + half), (slices + k, 8 + half, 8 + rows)):
            for j in range(blocks):
                sent_rows[spot : spot + 1, j * 128 : j * 128 + 128] = jnp.where(
                    odd, rows_pad[k, j, up : up + 1, :], rows_pad[k, j, low : low + 1, :]
                )

    def clear(ref, k):
        def one(i, carry):
            ref[k, i] = jnp.zeros(ref.shape[2:], jnp.float32)
            return carry

        lax.fori_loop(0, EXT, one, 0)

    for ok, k in ((far_ok, near_dst), (near_ok, far_dst)):
        @pl.when(jnp.logical_not(ok))
        def _(k=k):
            clear(ext, k)
            edges[k] = pad
    for ref, ok in ((from_right, right_ok), (from_left, left_ok)):
        @pl.when(jnp.logical_not(ok))
        def _(ref=ref):
            ref[...] = jnp.zeros(ref.shape, jnp.float32)

    def remote(src, dst, ssem, rsem, device, column):
        return pltpu.make_async_remote_copy(
            src_ref=src, dst_ref=dst, send_sem=ssem, recv_sem=rsem,
            device_id=(device, column), device_id_type=MESH,
        )

    def tile_of(q):
        return jnp.where(lax.rem(q, 2) == 1, (q + 1) // 2, GROUP - 1 - q // 2)

    def x_copy(q):
        span = pl.ds(tile_of(q) + 3, 1)
        return remote(
            sent.at[:, span], ext.at[pl.ds(own, slices), span],
            x_send.at[q], x_recv.at[q], partner, col,
        )

    def far_copy(q):
        span = pl.ds(tile_of(q) + 3, 1)
        return remote(
            ext.at[far_k, span], ext.at[far_dst, span],
            h_send.at[q], h_recv.at[q], far_d, col,
        )

    first_x = [
        remote(
            sent.at[:, pl.ds(at, 1)], ext.at[pl.ds(own, slices), pl.ds(at, 1)],
            x_send.at[i], x_recv.at[i], partner, col,
        )
        for i, at in ((0, 0), (CHUNKS, 3))
    ]
    first_x.append(
        remote(sent_rows, got_rows, x_send.at[CHUNKS + 1], x_recv.at[CHUNKS + 1], partner, col)
    )
    edge_x = remote(
        sent_edges, edges.at[pl.ds(own, slices)],
        x_send.at[CHUNKS + 2], x_recv.at[CHUNKS + 2], partner, col,
    )
    to_left = remote(own_edges, from_right, c_send.at[0], c_recv.at[0], d, col - 1)
    to_right = remote(own_edges, from_left, c_send.at[1], c_recv.at[1], d, col + 1)
    near = remote(
        ext.at[near_k], ext.at[near_dst], h_send.at[CHUNKS], h_recv.at[CHUNKS], near_d, col
    )
    near_edge = remote(
        edges.at[near_k], edges.at[near_dst],
        h_send.at[CHUNKS + 1], h_recv.at[CHUNKS + 1], near_d, col,
    )
    far_first = remote(
        ext.at[far_k, pl.ds(0, 4)], ext.at[far_dst, pl.ds(0, 4)],
        h_send.at[0], h_recv.at[0], far_d, col,
    )
    far_edge = remote(
        edges.at[far_k], edges.at[far_dst],
        h_send.at[CHUNKS + 2], h_recv.at[CHUNKS + 2], far_d, col,
    )

    pl.semaphore_wait(barrier, count)
    pl.when(left_ok)(to_left.start)
    pl.when(right_ok)(to_right.start)
    for copy in first_x:
        copy.start()
    x_copy(1).start()
    pl.when(near_ok)(near.start)
    pl.when(right_ok)(to_left.wait_recv)
    pl.when(left_ok)(to_right.wait_recv)
    for k in range(slices):
        even = jnp.bitwise_and(lane, 1) == 0
        edges[own + k] = jnp.where(even, from_right[k], from_left[k])
        sent_edges[k] = jnp.where(even, from_right[slices + k], from_left[slices + k])
    edge_x.start()
    pl.when(near_ok)(near_edge.start)

    def later(q, carry):
        x_copy(q).start()
        return carry

    lax.fori_loop(2, CHUNKS, later, 0)

    last_brick = order.shape[0] - 1
    ascending = jnp.broadcast_to(
        jnp.where(order[0] < order[last_brick], 1, 0), (8, cols)
    ) == 1
    row = lax.broadcasted_iota(jnp.int32, (8, cols), 0)

    def to_device(c):
        j, parity = c // 2, lax.rem(c, 2)
        return remote(
            part.at[c], inbox.at[parity, z], p_send.at[c], p_recv.at[parity, z],
            base + 2 * j + x, col,
        )

    def render(i, carry):
        @pl.when(i + 2 < CHUNKS)
        def _():
            x_copy(i + 2).wait_recv()

            @pl.when(far_ok)
            def _():
                far_copy(i + 2).start()

        @pl.when(jnp.logical_and(i + 1 < CHUNKS, near_ok))
        def _():
            far_copy(i + 1).wait_recv()

        c = jnp.where(lax.rem(i, 2) == 0, i // 2, GROUP - 1 - i // 2)
        acc = composite_tile(ext, halos, tab_ref, ascending, c, 2 * slices)
        mine = c // 2 == z

        @pl.when(mine)
        def _():
            for i in range(4):
                inbox[lax.rem(c, 2), z, i] = acc[i]

        @pl.when(jnp.logical_not(mine))
        def _():
            for i in range(4):
                part[c, i] = acc[i]
            to_device(c).start()

        return carry

    for copy in first_x:
        copy.wait_recv()
    for k in range(slices):
        above = pltpu.roll(ext[other + k, 0], 1, 0)
        below = pltpu.roll(ext[other + k, 3], 7, 0)
        ext[other + k, 2] = jnp.where(row == 0, got_rows[k : k + 1, :], above)
        ext[other + k, 1] = jnp.where(row == 7, got_rows[slices + k : slices + k + 1, :], below)
    pl.when(far_ok)(far_first.start)
    x_copy(1).wait_recv()
    pl.when(far_ok)(far_copy(1).start)
    edge_x.wait_recv()
    pl.when(far_ok)(far_edge.start)
    pl.when(far_ok)(near.wait_recv)
    pl.when(far_ok)(near_edge.wait_recv)
    pl.when(near_ok)(far_first.wait_recv)
    pl.when(near_ok)(far_edge.wait_recv)

    def unpack(k, carry):
        packed = edges[k]
        for at in range(EXT):
            halos[k, at] = pltpu.roll(packed, (128 - 2 * at) % 128, 1)
        return carry

    lax.fori_loop(0, end_k + 1, unpack, 0)
    lax.fori_loop(0, GROUP, render, 0)

    def gathered(parity):
        for j in range(GROUP // 2):
            @pl.when(z != j)
            def _(j=j):
                remote(
                    part.at[0], inbox.at[parity, j], p_send.at[0], p_recv.at[parity, j],
                    partner, col,
                ).wait_recv()
        acc = None
        for j in range(GROUP // 2):
            new = [inbox[parity, j, i] for i in range(4)]
            acc = new if acc is None else blend(ascending, acc, new)
        return acc

    for i, value in enumerate(gathered(1 - x)):
        last_out[i] = value
    last = remote(last_out, last_in, f_send, f_recv, partner, col)
    last.start()
    for i, value in enumerate(gathered(x)):
        out_ref[i, pl.ds(pl.multiple_of(8 * x, 8), 8), :] = value
    last.wait_recv()
    for i in range(4):
        out_ref[i, pl.ds(pl.multiple_of(8 - 8 * x, 8), 8), :] = last_in[i]

    last.wait_send()
    for copy in first_x + [edge_x]:
        copy.wait_send()
    for copy, ok in (
        (to_left, left_ok), (to_right, right_ok), (near, near_ok), (near_edge, near_ok),
        (far_first, far_ok), (far_edge, far_ok),
    ):
        pl.when(ok)(copy.wait_send)

    def drain_x(q, carry):
        x_copy(q).wait_send()

        @pl.when(far_ok)
        def _():
            far_copy(q).wait_send()

        return carry

    lax.fori_loop(1, CHUNKS, drain_x, 0)

    def drain(c, carry):
        @pl.when(c // 2 != z)
        def _():
            to_device(c).wait_send()

        return carry

    lax.fori_loop(0, GROUP, drain, 0)


def swap(x, bit):
    return lax.ppermute(x, "depth", [(i, i ^ bit) for i in range(lax.axis_size("depth"))])


def over(front, back, axis):
    alpha = lax.slice_in_dim(front, 3, 4, axis=axis)
    return front + (1.0 - alpha) * back


def body(voxel_bins, color_table, opacity_table, brick_order):
    me = lax.axis_index("depth")
    n = lax.axis_size("depth")
    slices, rows, cols = voxel_bins.shape
    tiles = rows // GROUP
    depth = 2 * slices + 2
    vmem = lambda *shape: pltpu.VMEM(shape, jnp.float32)
    dma = lambda *shape: pltpu.SemaphoreType.DMA(shape)
    picture = pl.pallas_call(
        functools.partial(render_kernel, n, lax.axis_size("col")),
        out_shape=jax.ShapeDtypeStruct((4, tiles, cols), jnp.float32),
        in_specs=[
            pl.BlockSpec(memory_space=pltpu.HBM),
            pl.BlockSpec(memory_space=pltpu.VMEM),
            pl.BlockSpec(memory_space=pltpu.VMEM),
            pl.BlockSpec(memory_space=pltpu.SMEM),
        ],
        out_specs=pl.BlockSpec(memory_space=pltpu.VMEM),
        scratch_shapes=[
            pltpu.VMEM((slices, rows, cols), jnp.int32),
            vmem(8, BINS),
            vmem(slices, cols // 128, rows + 16, 128),
            vmem(depth, EXT, 8, cols),
            vmem(depth, EXT, 8, 128),
            vmem(depth, 8, 128),
            vmem(2 * slices, 8, 128),
            vmem(2 * slices, 8, 128),
            vmem(2 * slices, 8, 128),
            vmem(slices, 8, 128),
            vmem(slices, EXT, 8, cols),
            vmem(2 * slices, cols),
            vmem(2 * slices, cols),
            vmem(GROUP, 4, 8, cols),
            vmem(2, GROUP // 2, 4, 8, cols),
            vmem(4, 8, cols),
            vmem(4, 8, cols),
            dma(slices),
            dma(CHUNKS + 3),
            dma(CHUNKS + 3),
            dma(CHUNKS + 3),
            dma(CHUNKS + 3),
            dma(2),
            dma(2),
            dma(GROUP),
            dma(2, GROUP // 2),
            pltpu.SemaphoreType.DMA,
            pltpu.SemaphoreType.DMA,
        ],
        compiler_params=pltpu.CompilerParams(
            collective_id=0, has_side_effects=True, vmem_limit_bytes=40 * 2**20
        ),
    )(voxel_bins, color_table, opacity_table[None], brick_order)
    ascending = brick_order[0] < brick_order[-1]
    return finish(picture, ascending, me, n)


def finish(picture, ascending, me, n):
    bit = GROUP
    while bit < n:
        count = picture.shape[1]
        halves = picture.reshape(4, count // 2, 2, picture.shape[2])
        set_bit = me // bit % 2 == 1
        keep = jnp.where(set_bit, halves[:, :, 1], halves[:, :, 0])
        got = swap(jnp.where(set_bit, halves[:, :, 0], halves[:, :, 1]), bit)
        picture = jnp.where(set_bit != ascending, over(keep, got, 0), over(got, keep, 0))
        bit *= 2
    return picture[:, :, None, :]


def solution(mesh):
    in_specs = (P("depth", None, "col"), P(), P(), P())
    out_specs = P(None, None, "depth", "col")
    return jax.shard_map(body, mesh=mesh, in_specs=in_specs, out_specs=out_specs, check_vma=False)
```
